128 devices in a mesh: tm: 128 (over y, x, z, core).
Axes of the slice: x: 4, y: 4, z: 4, core: 2. Of those that a mesh axis runs over, the one named last changes fastest.
Arguments:
- schur_inverse: float32 [128, 320, 320], P('tm'), as said below
- sweep_factor: float32 [128, 320, 320], P('tm')
Outputs:
- diagonal_blocks: float32 [128, 320, 320], P('tm')
- coupling_blocks: float32 [128, 320, 320], P('tm')
Inputs may be any that keep to these rules, and one draw needn't show every extreme that they name: Every block of schur_inverse is symmetric.
All inputs are finite; a program needn't handle non-finite values.
Results may differ from the reference program's by a relative error of at most 0.0003.
Values sent between devices are 32-bit elements; how exact they have to be, the bound alone decides.
No kernel may reach another device: no remote copies, remote signals or barrier semaphores. Data moves between devices by JAX's collectives and lax.ppermute only.
A program may use at most 192 MiB of HBM per device.

```python
import math
import jax
import jax.numpy as jnp
from jax import lax

B = 320
EPOCH_COUNT = 128


def product_high(left, right):
    return jnp.matmul(left, right, precision=lax.Precision.HIGHEST)


def joint_layout_profile(key):
    base_key = jax.random.fold_in(key, 101)
    stochastic_seeds = jax.random.split(base_key, 5)
    raw_matrix = jax.random.normal(stochastic_seeds[0], (B, B), jnp.float32)
    orthonormal_frame, _ = jnp.linalg.qr(raw_matrix)
    slow_share = 0.5
    reach = jax.random.uniform(stochastic_seeds[1], (B,), jnp.float32, 0.0, 0.5)
    slow_pick = jax.random.uniform(stochastic_seeds[2], (B,), jnp.float32, 0.0, 1.0) < slow_share
    fast_length = jnp.exp(jax.random.uniform(stochastic_seeds[3], (B,), jnp.float32, math.log(30.0), math.log(50.0)))
    lane_fading_speeds = jnp.where(slow_pick, 1.0 - reach / EPOCH_COUNT, 1.0 - 1.0 / fast_length)
    spike_indices = jax.random.randint(stochastic_seeds[4], (2,), 0, EPOCH_COUNT)
    return (orthonormal_frame, lane_fading_speeds, spike_indices)


def draw_schur_inverse(key, part):
    orthonormal_frame, lane_fading_speeds, spike_indices = joint_layout_profile(key)
    stochastic_seeds = jax.random.split(jax.random.fold_in(key, 7), 4)
    spread = 0.15 / math.sqrt(B)
    common_noise = jax.random.normal(stochastic_seeds[0], (B, B), jnp.float32) * spread
    common_noise = (common_noise + common_noise.T) * 0.7071
    own_noise = jax.random.normal(stochastic_seeds[1], (EPOCH_COUNT, B, B), jnp.float32) * spread
    own_noise = (own_noise + jnp.swapaxes(own_noise, 1, 2)) * 0.7071
    common_diag = jax.random.uniform(stochastic_seeds[2], (B,), jnp.float32, 0.7, 2.0)
    own_diag = jax.random.uniform(stochastic_seeds[3], (EPOCH_COUNT, B), jnp.float32, 0.9, 1.1)
    identity = jnp.eye(B, dtype=jnp.float32)
    inner = common_noise[None] + own_noise + identity[None] * (common_diag[None, :] * own_diag)[:, :, None]
    weight = jnp.sqrt(1.0 - lane_fading_speeds * lane_fading_speeds + 2.0 / EPOCH_COUNT)
    inner = inner * weight[None, :, None] * weight[None, None, :]
    blocks = product_high(product_high(orthonormal_frame[None], inner), orthonormal_frame.T[None])
    return 0.5 * (blocks + jnp.swapaxes(blocks, 1, 2))


def draw_sweep_factor(key, part):
    orthonormal_frame, lane_fading_speeds, spike_indices = joint_layout_profile(key)
    stochastic_seeds = jax.random.split(jax.random.fold_in(key, 11), 3)
    small_perturbation = jax.random.uniform(stochastic_seeds[0], (EPOCH_COUNT, B), jnp.float32, 0.0, 0.2) / EPOCH_COUNT
    magnitude_level = jax.random.uniform(stochastic_seeds[1], (EPOCH_COUNT, 1), jnp.float32, 0.75, 0.9)
    node_coordinates = jnp.arange(EPOCH_COUNT, dtype=jnp.int32)[:, None]
    spike_flag_grid = jnp.any(node_coordinates == spike_indices[None, :], axis=1)[:, None]
    increment_speeds = lane_fading_speeds[None, :] * (1.0 - small_perturbation) * jnp.where(spike_flag_grid, magnitude_level, 1.0)
    scaled_basis = orthonormal_frame[None, :, :] * increment_speeds[:, None, :]
    core = product_high(scaled_basis, orthonormal_frame.T[None])
    identity = jnp.eye(B, dtype=jnp.float32)
    tilt = identity[None] + jax.random.normal(stochastic_seeds[2], (EPOCH_COUNT, B, B), jnp.float32) * math.sqrt(0.15 / (B * EPOCH_COUNT))
    rotation, upper = jnp.linalg.qr(tilt)
    signs = jnp.sign(jnp.diagonal(upper, axis1=1, axis2=2))
    rotation = rotation * signs[:, None, :]
    return product_high(core, rotation)


def setup_inputs(seed: int = 0) -> dict:
    streams_of = jax.random.split(jax.random.key(seed), 3)
    schur_inverse = draw_schur_inverse(jax.random.fold_in(streams_of[2], 71), 0)
    sweep_factor = draw_sweep_factor(jax.random.fold_in(streams_of[2], 71), 0)
    return dict(schur_inverse=schur_inverse, sweep_factor=sweep_factor)


def matmul(left, right):
    return jnp.dot(left.astype(jnp.float32), right.astype(jnp.float32), precision=lax.Precision.HIGHEST, preferred_element_type=jnp.float32)

def reference(schur_inverse, sweep_factor):

    def advance(current, blocks):
        inverse, factor = blocks
        moved = matmul(factor, current)
        diagonal = inverse + matmul(moved, factor.T)
        return (diagonal, (diagonal, moved.T))
    start = jnp.zeros((B, B), jnp.float32)
    _, (diagonal_blocks, moved_rows) = lax.scan(advance, start, (schur_inverse, sweep_factor), reverse=True)
    coupling_blocks = jnp.concatenate([jnp.zeros((1, B, B), jnp.float32), moved_rows[:-1]], axis=0)
    return (diagonal_blocks, coupling_blocks)
```

```python
import functools

import jax
import jax.numpy as jnp
from jax import lax
from jax.experimental import pallas as pl
from jax.experimental.pallas import tpu as pltpu
from jax.sharding import PartitionSpec as P

TM = "tm"
F32 = jnp.float32
BF16 = jnp.bfloat16
B = 320
S_ROWS = 800
U_ROWS = 544


def index(y, x, z, core):
    return ((y * 4 + x) * 4 + z) * 2 + core


def route(axis, k):
    pairs = []
    for y in range(4):
        for x in range(4):
            for z in range(4):
                here = [y, x, z]
                there = [y, x, z]
                there[axis] = (there[axis] + k) % 4
                pairs.append((index(*there, 0), index(*here, 0)))
    return pairs


def route_later(k, last):
    return [
        (index(y + k, x, z, 0), index(y, x, z, 0))
        for y in range(4)
        for x in range(4)
        for z in range(4)
        if y + k <= last
    ]


CORES_DOWN = [(2 * chip + 1, 2 * chip) for chip in range(64)]
CORES_UP = [(2 * chip, 2 * chip + 1) for chip in range(64)]
NEXT = [(i, i + 1) for i in range(127)]


def send(value, pairs):
    return lax.ppermute(value, TM, pairs)


def split(a):
    high = a.astype(BF16)
    return high, (a - high.astype(F32)).astype(BF16)


def product(a, b):
    (ah, al), (bh, bl) = a, b
    return lax.dot_general(
        jnp.concatenate([ah, ah, al], axis=1),
        jnp.concatenate([bh, bl, bh], axis=0),
        (((1,), (0,)), ((), ())),
        preferred_element_type=F32,
    )


def product_t(a, b):
    (ah, al), (bh, bl) = a, b
    return lax.dot_general(
        jnp.concatenate([ah, ah, al], axis=1),
        jnp.concatenate([bh, bl, bh], axis=1),
        (((1,), (1,)), ((), ())),
        preferred_element_type=F32,
    )


def sandwich(a, middle):
    return product_t(split(product(a, split(middle))), a)


def unpack_s(ref):
    tail = ref[640:800, :]
    tail = jnp.concatenate([tail[:, :64], tail[:, 64:]], axis=0)
    return jnp.concatenate([ref[0:320, :], ref[320:640, :], tail], axis=1)


def pack_s(ref, a):
    ref[0:320, :] = a[:, 0:128]
    ref[320:640, :] = a[:, 128:256]
    ref[640:800, :] = jnp.concatenate([a[0:160, 256:320], a[160:320, 256:320]], axis=1)


def zeros(rows, columns):
    return jnp.zeros((rows, columns), F32)


def unpack_u(ref):
    b2 = ref[384:512, :]
    c2 = ref[512:544, :]
    c2 = jnp.concatenate([c2[:, :64], c2[:, 64:]], axis=0)
    top = jnp.concatenate([ref[0:128, :], ref[128:256, :], b2[:, :64]], axis=1)
    mid = jnp.concatenate([zeros(128, 128), ref[256:384, :], b2[:, 64:]], axis=1)
    low = jnp.concatenate([zeros(64, 256), c2], axis=1)
    return jnp.concatenate([top, mid, low], axis=0)


def upper_of(g):
    top = jnp.concatenate([0.5 * g[0:128, 0:128], g[0:128, 128:320]], axis=1)
    mid = jnp.concatenate([zeros(128, 128), 0.5 * g[128:256, 128:256], g[128:256, 256:320]], axis=1)
    low = jnp.concatenate([zeros(64, 256), 0.5 * g[256:320, 256:320]], axis=1)
    return jnp.concatenate([top, mid, low], axis=0)


def pack_u(ref, z):
    ref[0:128, :] = z[0:128, 0:128]
    ref[128:256, :] = z[0:128, 128:256] + z[128:256, 0:128].T
    ref[256:384, :] = z[128:256, 128:256]
    b02 = z[0:128, 256:320] + z[256:320, 0:128].T
    b12 = z[128:256, 256:320] + z[256:320, 128:256].T
    ref[384:512, :] = jnp.concatenate([b02, b12], axis=1)
    c = z[256:320, 256:320]
    ref[512:544, :] = jnp.concatenate([c[0:32], c[32:64]], axis=1)


def core_index():
    return lax.rem(lax.axis_index(TM), 2)


def place(axis):
    return lax.rem(lax.div(lax.axis_index(TM), (32, 8, 2)[axis]), 4)


def pair_s_kernel(own_ref, other_ref, s_ref):
    pack_s(s_ref, product(split(own_ref[...]), split(other_ref[...])))


def pair_u_kernel(l_ref, g_ref, other_ref, u_ref):
    pack_u(u_ref, upper_of(g_ref[...]) + sandwich(split(l_ref[...]), upper_of(other_ref[...])))


def load_slots(axis, refs, high, low):
    here = place(axis)
    for k, ref in enumerate(refs):
        slot = lax.rem(here + k, 4)
        high[slot], low[slot] = split(unpack_s(ref))
    return here


def chain_s_kernel(axis, s0, s1, s2, s3, total_ref, after_ref, high, low):
    here = load_slots(axis, (s0, s1, s2, s3), high, low)
    running = None
    for slot in (3, 2, 1, 0):
        factor = (high[slot], low[slot])
        if running is None:
            running = high[slot].astype(F32) + low[slot].astype(F32)
            row = lax.broadcasted_iota(jnp.int32, (B, B), 0)
            column = lax.broadcasted_iota(jnp.int32, (B, B), 1)

            @pl.when(here == 3)
            def _():
                pack_s(after_ref, jnp.where(row == column, 1.0, 0.0).astype(F32))
        else:
            running = product(factor, split(running))
        if slot > 0:
            kept = running

            @pl.when(here == slot - 1)
            def _():
                pack_s(after_ref, kept)
    pack_s(total_ref, running)


def chain_u_kernel(axis, s0, s1, s2, s3, u0, u1, u2, u3, total_ref, after_ref, high, low, middle):
    here = load_slots(axis, (s0, s1, s2, s3), high, low)
    for k, ref in enumerate((u0, u1, u2, u3)):
        middle[lax.rem(here + k, 4)] = unpack_u(ref)

    @pl.when(here == 3)
    def _():
        after_ref[...] = jnp.zeros((B, B), F32)

    running = middle[3]
    for slot in (2, 1, 0):
        kept = running

        @pl.when(here == slot)
        def _():
            after_ref[...] = kept

        running = middle[slot] + sandwich((high[slot], low[slot]), running)
    pack_u(total_ref, running)


def own_kernel(s_ref, l_ref, u_ref, g_ref, p0_ref, p1_ref, z0_ref, z1_ref, ap_ref, o_ref, high, low, base, p, z):
    core = core_index()

    @pl.when(core == 0)
    def _():
        high[...], low[...] = split(unpack_s(s_ref))
        base[...] = unpack_u(u_ref)
        p[...] = unpack_s(p0_ref)
        z[...] = z0_ref[...]

    @pl.when(core != 0)
    def _():
        high[...], low[...] = split(l_ref[...])
        base[...] = upper_of(g_ref[...])
        p[...] = unpack_s(p1_ref)
        z[...] = z1_ref[...]

    a = (high[...], low[...])
    ap_ref[...] = product(a, split(p[...]))
    o_ref[...] = base[...] + sandwich(a, z[...])


def reach_kernel(ap_ref, p0_ref, p1_ref, a0_ref, a1_ref, b0_ref, b1_ref, r1_ref, r2_ref, r3_ref, p, a, b):
    core = core_index()

    @pl.when(core == 0)
    def _():
        p[...] = unpack_s(p0_ref)
        a[...] = unpack_s(a0_ref)
        b[...] = unpack_s(b0_ref)

    @pl.when(core != 0)
    def _():
        p[...] = unpack_s(p1_ref)
        a[...] = unpack_s(a1_ref)
        b[...] = unpack_s(b1_ref)

    r1 = product(split(ap_ref[...]), split(p[...]))
    r2 = product(split(r1), split(a[...]))
    r1_ref[...] = r1
    r2_ref[...] = r2
    r3_ref[...] = product(split(r2), split(b[...]))


def first_kernel(o_ref, ap_ref, z0_ref, z1_ref, r1_ref, u0_ref, u1_ref, r3_ref, w0_ref, w1_ref, acc_ref, z, u, w):
    core = core_index()

    @pl.when(core == 0)
    def _():
        z[...] = z0_ref[...]
        u[...] = unpack_u(u0_ref)
        w[...] = unpack_u(w0_ref)

    @pl.when(core != 0)
    def _():
        z[...] = z1_ref[...]
        u[...] = unpack_u(u1_ref)
        w[...] = unpack_u(w1_ref)

    acc = o_ref[...] + sandwich(split(ap_ref[...]), z[...])
    acc = acc + sandwich(split(r1_ref[...]), u[...])
    acc_ref[...] = acc + sandwich(split(r3_ref[...]), w[...])


def last_kernel(acc_ref, r2_ref, u0_ref, u1_ref, before_ref, x_ref, c_ref, u):
    core = core_index()

    @pl.when(core == 0)
    def _():
        u[...] = unpack_u(u0_ref)

    @pl.when(core != 0)
    def _():
        u[...] = unpack_u(u1_ref)

    half = acc_ref[...] + sandwich(split(r2_ref[...]), u[...])
    x = half + half.T
    x_ref[0] = x
    c_ref[0] = product_t(split(x), split(before_ref[...]))


def run(kernel, shapes, scratch, products, *operands):
    size = sum(o.size for o in operands) * 4
    return pl.pallas_call(
        kernel,
        out_shape=[jax.ShapeDtypeStruct(s, F32) for s in shapes],
        scratch_shapes=[pltpu.VMEM(s, d) for s, d in scratch],
        compiler_params=pltpu.CompilerParams(vmem_limit_bytes=32 * 1024 * 1024),
        cost_estimate=pl.CostEstimate(flops=products * 6 * B**3, bytes_accessed=size, transcendentals=0),
    )(*operands)


S_SHAPE = (S_ROWS, 128)
U_SHAPE = (U_ROWS, 128)
FULL = (B, B)
SLOTS = [((4, B, B), BF16), ((4, B, B), BF16)]


def local(schur_inverse, sweep_factor):
    g, l = schur_inverse[0], sweep_factor[0]

    l_other = send(l, CORES_DOWN)
    g_other = send(g, CORES_DOWN)
    (s,) = run(pair_s_kernel, [S_SHAPE], [], 1, l, l_other)
    (u,) = run(pair_u_kernel, [U_SHAPE], [], 2, l, g, g_other)

    s_z = [send(s, route(2, k)) for k in (1, 2, 3)]
    u_z = [send(u, route(2, k)) for k in (1, 2, 3)]
    line_s, after_s_z = run(functools.partial(chain_s_kernel, 2), [S_SHAPE, S_SHAPE], SLOTS, 3, s, *s_z)
    s_x = [send(line_s, route(1, k)) for k in (1, 2, 3)]
    line_u, after_u_z = run(
        functools.partial(chain_u_kernel, 2), [U_SHAPE, FULL], SLOTS + [((4, B, B), F32)], 6, s, *s_z, u, *u_z
    )

    u_x = [send(line_u, route(1, k)) for k in (1, 2, 3)]
    plane_s, after_s_x = run(functools.partial(chain_s_kernel, 1), [S_SHAPE, S_SHAPE], SLOTS, 3, line_s, *s_x)
    s_y = [send(plane_s, route_later(k, 2)) for k in (1, 2)]
    plane_u, after_u_x = run(
        functools.partial(chain_u_kernel, 1), [U_SHAPE, FULL], SLOTS + [((4, B, B), F32)], 6, line_s, *s_x, line_u, *u_x
    )

    u_y = [send(plane_u, route_later(k, 3)) for k in (1, 2, 3)]

    before = send(l, NEXT)
    ap, o = run(
        own_kernel,
        [FULL, FULL],
        [(FULL, BF16), (FULL, BF16), (FULL, F32), (FULL, F32), (FULL, F32)],
        3,
        s, l, u, g, after_s_z, send(after_s_z, CORES_UP), after_u_z, send(after_u_z, CORES_UP),
    )
    r1, r2, r3 = run(
        reach_kernel,
        [FULL, FULL, FULL],
        [(FULL, F32)] * 3,
        3,
        ap, after_s_x, send(after_s_x, CORES_UP), s_y[0], send(s_y[0], CORES_UP), s_y[1], send(s_y[1], CORES_UP),
    )
    (acc,) = run(
        first_kernel,
        [FULL],
        [(FULL, F32)] * 3,
        6,
        o, ap, after_u_x, send(after_u_x, CORES_UP), r1, u_y[0], send(u_y[0], CORES_UP),
        r3, u_y[2], send(u_y[2], CORES_UP),
    )
    return tuple(
        run(
            last_kernel,
            [(1, B, B), (1, B, B)],
            [(FULL, F32)],
            3,
            acc, r2, u_y[1], send(u_y[1], CORES_UP), before,
        )
    )


def solution(mesh):
    spec = P(TM, None, None)
    return jax.shard_map(local, mesh=mesh, in_specs=(spec, spec), out_specs=(spec, spec), check_vma=False)
```

```python
import functools

import jax
import jax.numpy as jnp
from jax import lax
from jax.experimental import pallas as pl
from jax.experimental.pallas import tpu as pltpu
from jax.sharding import PartitionSpec as P

TM = "tm"
F32 = jnp.float32
BF16 = jnp.bfloat16
B = 320
S_ROWS = 800
U_ROWS = 544


def index(y, x, z, core):
    return ((y * 4 + x) * 4 + z) * 2 + core


def moved(axis, k_of_core):
    pairs = []
    for y in range(4):
        for x in range(4):
            for z in range(4):
                for core in range(2):
                    there = [y, x, z]
                    there[axis] = (there[axis] + k_of_core[core]) % 4
                    pairs.append((index(*there, core), index(y, x, z, core)))
    return pairs


CORES = [(i, i ^ 1) for i in range(128)]
NEXT = [(i, (i + 1) % 128) for i in range(128)]


def send(value, pairs):
    return lax.ppermute(value, TM, pairs)


def split(a):
    high = a.astype(BF16)
    return high, (a - high.astype(F32)).astype(BF16)


def product(a, b):
    (ah, al), (bh, bl) = a, b
    return lax.dot_general(
        jnp.concatenate([ah, ah, al], axis=1),
        jnp.concatenate([bh, bl, bh], axis=0),
        (((1,), (0,)), ((), ())),
        preferred_element_type=F32,
    )


def product_t(a, b):
    (ah, al), (bh, bl) = a, b
    return lax.dot_general(
        jnp.concatenate([ah, ah, al], axis=1),
        jnp.concatenate([bh, bl, bh], axis=1),
        (((1,), (1,)), ((), ())),
        preferred_element_type=F32,
    )


def sandwich(a, middle):
    return product_t(split(product(a, split(middle))), a)


def unpack_s(ref):
    tail = ref[640:800, :]
    tail = jnp.concatenate([tail[:, :64], tail[:, 64:]], axis=0)
    return jnp.concatenate([ref[0:320, :], ref[320:640, :], tail], axis=1)


def pack_s(ref, a):
    ref[0:320, :] = a[:, 0:128]
    ref[320:640, :] = a[:, 128:256]
    ref[640:800, :] = jnp.concatenate([a[0:160, 256:320], a[160:320, 256:320]], axis=1)


def zeros(rows, columns):
    return jnp.zeros((rows, columns), F32)


def unpack_u(ref):
    b2 = ref[384:512, :]
    c2 = ref[512:544, :]
    c2 = jnp.concatenate([c2[:, :64], c2[:, 64:]], axis=0)
    top = jnp.concatenate([ref[0:128, :], ref[128:256, :], b2[:, :64]], axis=1)
    mid = jnp.concatenate([zeros(128, 128), ref[256:384, :], b2[:, 64:]], axis=1)
    low = jnp.concatenate([zeros(64, 256), c2], axis=1)
    return jnp.concatenate([top, mid, low], axis=0)


def upper_of(g):
    top = jnp.concatenate([0.5 * g[0:128, 0:128], g[0:128, 128:320]], axis=1)
    mid = jnp.concatenate([zeros(128, 128), 0.5 * g[128:256, 128:256], g[128:256, 256:320]], axis=1)
    low = jnp.concatenate([zeros(64, 256), 0.5 * g[256:320, 256:320]], axis=1)
    return jnp.concatenate([top, mid, low], axis=0)


def pack_u(ref, z):
    ref[0:128, :] = z[0:128, 0:128]
    ref[128:256, :] = z[0:128, 128:256] + z[128:256, 0:128].T
    ref[256:384, :] = z[128:256, 128:256]
    b02 = z[0:128, 256:320] + z[256:320, 0:128].T
    b12 = z[128:256, 256:320] + z[256:320, 128:256].T
    ref[384:512, :] = jnp.concatenate([b02, b12], axis=1)
    c = z[256:320, 256:320]
    ref[512:544, :] = jnp.concatenate([c[0:32], c[32:64]], axis=1)


def core_index():
    return lax.rem(lax.axis_index(TM), 2)


def place(axis):
    return lax.rem(lax.div(lax.axis_index(TM), (32, 8, 2)[axis]), 4)


def half_of(ref, rows):
    return ref[pl.ds(pl.multiple_of(core_index() * (rows // 2), 8), rows // 2), :]


def join(out, mine, other):
    rows = mine.shape[0]
    core = core_index()
    out[pl.ds(pl.multiple_of(core * rows, 8), rows), :] = mine[...]
    out[pl.ds(pl.multiple_of((1 - core) * rows, 8), rows), :] = other[...]


def ring_slots(axis):
    here = place(axis)
    turn = 2 * core_index()
    return [lax.rem(here + k, 4) for k in (0, 1 + turn, 3 - turn, 2)]


def pair_kernel(l_ref, l_other_ref, g_ref, g_other_ref, s_ref, s_half_ref, u_ref, u_half_ref):
    core = core_index()
    own, other = l_ref[...], l_other_ref[...]
    first = split(jnp.where(core == 0, own, other))
    second = split(jnp.where(core == 0, other, own))
    pack_s(s_ref, product(first, second))
    s_half_ref[...] = half_of(s_ref, S_ROWS)
    own, other = g_ref[...], g_other_ref[...]
    start = jnp.where(core == 0, own, other)
    later = jnp.where(core == 0, other, own)
    pack_u(u_ref, upper_of(start) + sandwich(first, upper_of(later)))
    u_half_ref[...] = half_of(u_ref, U_ROWS)


def load_s(axis, s, mine, other, mine_half, other_half, high, low, whole):
    join(whole, mine_half, other_half)
    for slot, ref in zip(ring_slots(axis), (s, mine, other, whole)):
        high[slot], low[slot] = split(unpack_s(ref))


def chain_s_kernel(axis, s0, s1, s2, s3, s4, total_ref, half_ref, after_ref, high, low, whole):
    load_s(axis, s0, s1, s2, s3, s4, high, low, whole)
    here = place(axis)
    running = None
    for slot in (3, 2, 1, 0):
        factor = (high[slot], low[slot])
        if running is None:
            running = high[slot].astype(F32) + low[slot].astype(F32)
            row = lax.broadcasted_iota(jnp.int32, (B, B), 0)
            column = lax.broadcasted_iota(jnp.int32, (B, B), 1)

            @pl.when(here == 3)
            def _():
                after_ref[...] = jnp.where(row == column, 1.0, 0.0).astype(F32)
        else:
            running = product(factor, split(running))
        if slot > 0:
            kept = running

            @pl.when(here == slot - 1)
            def _():
                after_ref[...] = kept

    pack_s(total_ref, running)
    half_ref[...] = half_of(total_ref, S_ROWS)


def chain_u_kernel(
    axis, s0, s1, s2, s3, s4, u0, u1, u2, u3, u4, _, total_ref, half_ref, after_ref, high, low, whole, middle, whole_u
):
    load_s(axis, s0, s1, s2, s3, s4, high, low, whole)
    join(whole_u, u3, u4)
    for slot, ref in zip(ring_slots(axis), (u0, u1, u2, whole_u)):
        middle[slot] = unpack_u(ref)
    here = place(axis)

    @pl.when(here == 3)
    def _():
        after_ref[...] = jnp.zeros((B, B), F32)

    running = middle[3]
    for slot in (2, 1, 0):
        kept = running

        @pl.when(here == slot)
        def _():
            after_ref[...] = kept

        running = middle[slot] + sandwich((high[slot], low[slot]), running)
    pack_u(total_ref, running)
    half_ref[...] = half_of(total_ref, U_ROWS)


def own_kernel(s_ref, l_ref, u_ref, g_ref, p_ref, z_ref, ap_ref, o_ref, packed_ref, high, low, base):
    core = core_index()
    pack_s(packed_ref, l_ref[...])

    @pl.when(core == 0)
    def _():
        high[...], low[...] = split(unpack_s(s_ref))
        base[...] = unpack_u(u_ref)

    @pl.when(core != 0)
    def _():
        high[...], low[...] = split(l_ref[...])
        base[...] = upper_of(g_ref[...])

    a = (high[...], low[...])
    ap_ref[...] = product(a, split(p_ref[...]))
    o_ref[...] = base[...] + sandwich(a, z_ref[...])


def reach_kernel(o_ref, ap_ref, p_ref, z_ref, mine_ref, other_ref, acc_ref, r1_ref, r2_ref, r3_ref, a, b):
    core = core_index()
    y = place(0)

    @pl.when(core == 0)
    def _():
        a[...] = unpack_s(mine_ref)
        b[...] = unpack_s(other_ref)

    @pl.when(core != 0)
    def _():
        a[...] = unpack_s(other_ref)
        b[...] = unpack_s(mine_ref)

    ap = split(ap_ref[...])
    acc_ref[...] = o_ref[...] + sandwich(ap, z_ref[...])
    r1 = jnp.where(y < 3, product(ap, split(p_ref[...])), 0.0)
    r2 = jnp.where(y < 2, product(split(r1), split(a[...])), 0.0)
    r3 = jnp.where(y < 1, product(split(r2), split(b[...])), 0.0)
    r1_ref[...] = r1
    r2_ref[...] = r2
    r3_ref[...] = r3


def last_kernel(acc_ref, r1_ref, r2_ref, r3_ref, mine_ref, other_ref, mine_half, other_half, before_ref, x_ref, c_ref, u, w, whole):
    core = core_index()

    @pl.when(core == 0)
    def _():
        u[...] = unpack_u(mine_ref)
        w[...] = unpack_u(other_ref)

    @pl.when(core != 0)
    def _():
        u[...] = unpack_u(other_ref)
        w[...] = unpack_u(mine_ref)

    join(whole, mine_half, other_half)
    half = acc_ref[...] + sandwich(split(r1_ref[...]), u[...]) + sandwich(split(r3_ref[...]), w[...])
    half = half + sandwich(split(r2_ref[...]), unpack_u(whole))
    x = half + half.T
    x_ref[0] = x
    before = jnp.where(lax.axis_index(TM) > 0, unpack_s(before_ref), 0.0)
    c_ref[0] = product_t(split(x), split(before))


def run(kernel, shapes, scratch, products, *operands, after=()):
    size = sum(o.size for o in operands) * 4
    specs = [pl.BlockSpec(memory_space=pltpu.VMEM)] * len(operands) + [pl.BlockSpec(memory_space=pl.ANY)] * len(after)
    return pl.pallas_call(
        kernel,
        in_specs=specs,
        out_shape=[jax.ShapeDtypeStruct(s, F32) for s in shapes],
        scratch_shapes=[pltpu.VMEM(s, d) for s, d in scratch],
        compiler_params=pltpu.CompilerParams(vmem_limit_bytes=32 * 1024 * 1024),
        cost_estimate=pl.CostEstimate(flops=10**9, bytes_accessed=10**7, transcendentals=0),
    )(*operands, *after)


S_SHAPE = (S_ROWS, 128)
S_HALF = (S_ROWS // 2, 128)
U_SHAPE = (U_ROWS, 128)
U_HALF = (U_ROWS // 2, 128)
FULL = (B, B)
S_SLOTS = [((4, B, B), BF16), ((4, B, B), BF16), (S_SHAPE, F32)]
U_SLOTS = S_SLOTS + [((4, B, B), F32), (U_SHAPE, F32)]


def ring(axis, whole, half):
    return send(whole, moved(axis, (1, 3))), send(half, moved(axis, (2, 2)))


def exchanged(mine, mine_half):
    return mine, send(mine, CORES), mine_half, send(mine_half, CORES)


def local(schur_inverse, sweep_factor):
    g, l = schur_inverse[0], sweep_factor[0]

    l_other = send(l, CORES)
    g_other = send(g, CORES)
    s, s_half, u, u_half = run(pair_kernel, [S_SHAPE, S_HALF, U_SHAPE, U_HALF], [], 3, l, l_other, g, g_other)

    s_z = ring(2, s, s_half)
    u_z = ring(2, u, u_half)
    s_z = exchanged(*s_z)
    line_s, line_s_half, p_z = run(functools.partial(chain_s_kernel, 2), [S_SHAPE, S_HALF, FULL], S_SLOTS, 3, s, *s_z)
    s_x = ring(1, line_s, line_s_half)
    u_z = exchanged(*u_z)
    line_u, line_u_half, q_z = run(
        functools.partial(chain_u_kernel, 2), [U_SHAPE, U_HALF, FULL], U_SLOTS, 6, s, *s_z, u, *u_z, after=(line_s,)
    )

    u_x = ring(1, line_u, line_u_half)
    s_x = exchanged(*s_x)
    ap, o, packed = run(own_kernel, [FULL, FULL, S_SHAPE], [(FULL, BF16), (FULL, BF16), (FULL, F32)], 3, s, l, u, g, p_z, q_z)
    plane_s, _, p_x = run(functools.partial(chain_s_kernel, 1), [S_SHAPE, S_HALF, FULL], S_SLOTS, 3, line_s, *s_x)
    s_y = send(plane_s, moved(0, (1, 2)))
    before = send(packed, NEXT)
    u_x = exchanged(*u_x)
    plane_u, plane_u_half, q_x = run(
        functools.partial(chain_u_kernel, 1),
        [U_SHAPE, U_HALF, FULL],
        U_SLOTS,
        6,
        line_s, *s_x, line_u, *u_x,
        after=(ap,),
    )

    u_y = ring(0, plane_u, plane_u_half)
    s_y_other = send(s_y, CORES)
    u_1, u_1_other, u_2, u_2_other = exchanged(*u_y)
    acc, r1, r2, r3 = run(reach_kernel, [FULL] * 4, [(FULL, F32)] * 2, 5, o, ap, p_x, q_x, s_y, s_y_other)
    return tuple(
        run(
            last_kernel,
            [(1, B, B), (1, B, B)],
            [(FULL, F32), (FULL, F32), (U_SHAPE, F32)],
            7,
            acc, r1, r2, r3, u_1, u_1_other, u_2, u_2_other, before,
        )
    )


def solution(mesh):
    spec = P(TM, None, None)
    return jax.shard_map(local, mesh=mesh, in_specs=(spec, spec), out_specs=(spec, spec), check_vma=False)
```

```python
import functools

import jax
import jax.numpy as jnp
from jax import lax
from jax.experimental import pallas as pl
from jax.experimental.pallas import tpu as pltpu
from jax.sharding import PartitionSpec as P

TM = "tm"
F32 = jnp.float32
BF16 = jnp.bfloat16
B = 320
S_ROWS = 800
U_ROWS = 544


def index(y, x, z, core):
    return ((y * 4 + x) * 4 + z) * 2 + core


def moved(axis, k_of_core):
    pairs = []
    for y in range(4):
        for x in range(4):
            for z in range(4):
                for core in range(2):
                    there = [y, x, z]
                    there[axis] = (there[axis] + k_of_core[core]) % 4
                    pairs.append((index(*there, core), index(y, x, z, core)))
    return pairs


CORES = [(i, i ^ 1) for i in range(128)]
NEXT = [(i, (i + 1) % 128) for i in range(128)]


def send(value, pairs):
    return lax.ppermute(value, TM, pairs)


def split(a):
    high = a.astype(BF16)
    return high, (a - high.astype(F32)).astype(BF16)


def product(a, b):
    (ah, al), (bh, bl) = a, b
    return lax.dot_general(
        jnp.concatenate([ah, ah, al], axis=1),
        jnp.concatenate([bh, bl, bh], axis=0),
        (((1,), (0,)), ((), ())),
        preferred_element_type=F32,
    )


def product_t(a, b):
    (ah, al), (bh, bl) = a, b
    return lax.dot_general(
        jnp.concatenate([ah, ah, al], axis=1),
        jnp.concatenate([bh, bl, bh], axis=1),
        (((1,), (1,)), ((), ())),
        preferred_element_type=F32,
    )


def sandwich(a, middle):
    return product_t(split(product(a, split(middle))), a)


def unpack_s(ref):
    tail = ref[640:800, :]
    tail = jnp.concatenate([tail[:, :64], tail[:, 64:]], axis=0)
    return jnp.concatenate([ref[0:320, :], ref[320:640, :], tail], axis=1)


def pack_s(ref, a):
    ref[0:320, :] = a[:, 0:128]
    ref[320:640, :] = a[:, 128:256]
    ref[640:800, :] = jnp.concatenate([a[0:160, 256:320], a[160:320, 256:320]], axis=1)


def zeros(rows, columns):
    return jnp.zeros((rows, columns), F32)


def unpack_u(ref):
    b2 = ref[384:512, :]
    c2 = ref[512:544, :]
    c2 = jnp.concatenate([c2[:, :64], c2[:, 64:]], axis=0)
    top = jnp.concatenate([ref[0:128, :], ref[128:256, :], b2[:, :64]], axis=1)
    mid = jnp.concatenate([zeros(128, 128), ref[256:384, :], b2[:, 64:]], axis=1)
    low = jnp.concatenate([zeros(64, 256), c2], axis=1)
    return jnp.concatenate([top, mid, low], axis=0)


def upper_of(g):
    top = jnp.concatenate([0.5 * g[0:128, 0:128], g[0:128, 128:320]], axis=1)
    mid = jnp.concatenate([zeros(128, 128), 0.5 * g[128:256, 128:256], g[128:256, 256:320]], axis=1)
    low = jnp.concatenate([zeros(64, 256), 0.5 * g[256:320, 256:320]], axis=1)
    return jnp.concatenate([top, mid, low], axis=0)


def pack_u(ref, z):
    ref[0:128, :] = z[0:128, 0:128]
    ref[128:256, :] = z[0:128, 128:256] + z[128:256, 0:128].T
    ref[256:384, :] = z[128:256, 128:256]
    b02 = z[0:128, 256:320] + z[256:320, 0:128].T
    b12 = z[128:256, 256:320] + z[256:320, 128:256].T
    ref[384:512, :] = jnp.concatenate([b02, b12], axis=1)
    c = z[256:320, 256:320]
    ref[512:544, :] = jnp.concatenate([c[0:32], c[32:64]], axis=1)


def core_index():
    return lax.rem(lax.axis_index(TM), 2)


def place(axis):
    return lax.rem(lax.div(lax.axis_index(TM), (32, 8, 2)[axis]), 4)


def half_of(ref, rows):
    return ref[pl.ds(pl.multiple_of(core_index() * (rows // 2), 8), rows // 2), :]


def join(out, mine, other):
    rows = mine.shape[0]
    core = core_index()
    out[pl.ds(pl.multiple_of(core * rows, 8), rows), :] = mine[...]
    out[pl.ds(pl.multiple_of((1 - core) * rows, 8), rows), :] = other[...]


def ring_slots(axis):
    here = place(axis)
    core = core_index()
    return [lax.rem(here + k, 4) for k in (0, 1 + core, 2 - core, 3)]


def pair_kernel(l_ref, l_other_ref, g_ref, g_other_ref, s_ref, s_half_ref, u_ref, u_half_ref):
    core = core_index()
    own, other = l_ref[...], l_other_ref[...]
    first = split(jnp.where(core == 0, own, other))
    second = split(jnp.where(core == 0, other, own))
    pack_s(s_ref, product(first, second))
    s_half_ref[...] = half_of(s_ref, S_ROWS)
    own, other = g_ref[...], g_other_ref[...]
    start = jnp.where(core == 0, own, other)
    later = jnp.where(core == 0, other, own)
    pack_u(u_ref, upper_of(start) + sandwich(first, upper_of(later)))
    u_half_ref[...] = half_of(u_ref, U_ROWS)


def load_s(axis, s, mine, other, mine_half, other_half, high, low, whole):
    join(whole, mine_half, other_half)
    for slot, ref in zip(ring_slots(axis), (s, mine, other, whole)):
        high[slot], low[slot] = split(unpack_s(ref))


def chain_s_kernel(axis, s0, s1, s2, s3, s4, total_ref, half_ref, after_ref, high, low, whole):
    load_s(axis, s0, s1, s2, s3, s4, high, low, whole)
    here = place(axis)
    running = None
    for slot in (3, 2, 1, 0):
        factor = (high[slot], low[slot])
        if running is None:
            running = high[slot].astype(F32) + low[slot].astype(F32)
            row = lax.broadcasted_iota(jnp.int32, (B, B), 0)
            column = lax.broadcasted_iota(jnp.int32, (B, B), 1)

            @pl.when(here == 3)
            def _():
                after_ref[...] = jnp.where(row == column, 1.0, 0.0).astype(F32)
        else:
            running = product(factor, split(running))
        if slot > 0:
            kept = running

            @pl.when(here == slot - 1)
            def _():
                after_ref[...] = kept

    pack_s(total_ref, running)
    half_ref[...] = half_of(total_ref, S_ROWS)


def chain_u_kernel(
    axis, s0, s1, s2, s3, s4, u0, u1, u2, u3, u4, _, total_ref, half_ref, after_ref, high, low, whole, middle, whole_u
):
    load_s(axis, s0, s1, s2, s3, s4, high, low, whole)
    join(whole_u, u3, u4)
    for slot, ref in zip(ring_slots(axis), (u0, u1, u2, whole_u)):
        middle[slot] = unpack_u(ref)
    here = place(axis)

    @pl.when(here == 3)
    def _():
        after_ref[...] = jnp.zeros((B, B), F32)

    running = middle[3]
    for slot in (2, 1, 0):
        kept = running

        @pl.when(here == slot)
        def _():
            after_ref[...] = kept

        running = middle[slot] + sandwich((high[slot], low[slot]), running)
    pack_u(total_ref, running)
    half_ref[...] = half_of(total_ref, U_ROWS)


def own_kernel(s_ref, l_ref, u_ref, g_ref, p_ref, z_ref, ap_ref, o_ref, packed_ref, high, low, base):
    core = core_index()
    pack_s(packed_ref, l_ref[...])

    @pl.when(core == 0)
    def _():
        high[...], low[...] = split(unpack_s(s_ref))
        base[...] = unpack_u(u_ref)

    @pl.when(core != 0)
    def _():
        high[...], low[...] = split(l_ref[...])
        base[...] = upper_of(g_ref[...])

    a = (high[...], low[...])
    ap_ref[...] = product(a, split(p_ref[...]))
    o_ref[...] = base[...] + sandwich(a, z_ref[...])


def reach_kernel(o_ref, ap_ref, p_ref, z_ref, mine_ref, other_ref, acc_ref, r1_ref, r2_ref, r3_ref, a, b):
    core = core_index()
    y = place(0)

    @pl.when(core == 0)
    def _():
        a[...] = unpack_s(mine_ref)
        b[...] = unpack_s(other_ref)

    @pl.when(core != 0)
    def _():
        a[...] = unpack_s(other_ref)
        b[...] = unpack_s(mine_ref)

    ap = split(ap_ref[...])
    acc_ref[...] = o_ref[...] + sandwich(ap, z_ref[...])
    r1 = jnp.where(y < 3, product(ap, split(p_ref[...])), 0.0)
    r2 = jnp.where(y < 2, product(split(r1), split(a[...])), 0.0)
    r3 = jnp.where(y < 1, product(split(r2), split(b[...])), 0.0)
    r1_ref[...] = r1
    r2_ref[...] = r2
    r3_ref[...] = r3


def last_kernel(acc_ref, r1_ref, r2_ref, r3_ref, mine_ref, other_ref, mine_half, other_half, before_ref, x_ref, c_ref, u, w, whole):
    core = core_index()

    @pl.when(core == 0)
    def _():
        u[...] = unpack_u(mine_ref)
        w[...] = unpack_u(other_ref)

    @pl.when(core != 0)
    def _():
        u[...] = unpack_u(other_ref)
        w[...] = unpack_u(mine_ref)

    join(whole, mine_half, other_half)
    half = acc_ref[...] + sandwich(split(r1_ref[...]), u[...]) + sandwich(split(r2_ref[...]), w[...])
    half = half + sandwich(split(r3_ref[...]), unpack_u(whole))
    x = half + half.T
    x_ref[0] = x
    before = jnp.where(lax.axis_index(TM) > 0, unpack_s(before_ref), 0.0)
    c_ref[0] = product_t(split(x), split(before))


def run(kernel, shapes, scratch, products, *operands, after=()):
    size = sum(o.size for o in operands) * 4
    specs = [pl.BlockSpec(memory_space=pltpu.VMEM)] * len(operands) + [pl.BlockSpec(memory_space=pl.ANY)] * len(after)
    return pl.pallas_call(
        kernel,
        in_specs=specs,
        out_shape=[jax.ShapeDtypeStruct(s, F32) for s in shapes],
        scratch_shapes=[pltpu.VMEM(s, d) for s, d in scratch],
        compiler_params=pltpu.CompilerParams(vmem_limit_bytes=32 * 1024 * 1024),
        cost_estimate=pl.CostEstimate(flops=10**9, bytes_accessed=10**7, transcendentals=0),
    )(*operands, *after)


S_SHAPE = (S_ROWS, 128)
S_HALF = (S_ROWS // 2, 128)
U_SHAPE = (U_ROWS, 128)
U_HALF = (U_ROWS // 2, 128)
FULL = (B, B)
S_SLOTS = [((4, B, B), BF16), ((4, B, B), BF16), (S_SHAPE, F32)]
U_SLOTS = S_SLOTS + [((4, B, B), F32), (U_SHAPE, F32)]


def ring(axis, whole, half):
    return send(whole, moved(axis, (1, 2))), send(half, moved(axis, (3, 3)))


def exchanged(mine, mine_half):
    return mine, send(mine, CORES), mine_half, send(mine_half, CORES)


def local(schur_inverse, sweep_factor):
    g, l = schur_inverse[0], sweep_factor[0]

    l_other = send(l, CORES)
    g_other = send(g, CORES)
    s, s_half, u, u_half = run(pair_kernel, [S_SHAPE, S_HALF, U_SHAPE, U_HALF], [], 3, l, l_other, g, g_other)

    s_z = ring(2, s, s_half)
    u_z = ring(2, u, u_half)
    s_z = exchanged(*s_z)
    line_s, line_s_half, p_z = run(functools.partial(chain_s_kernel, 2), [S_SHAPE, S_HALF, FULL], S_SLOTS, 3, s, *s_z)
    s_x = ring(1, line_s, line_s_half)
    u_z = exchanged(*u_z)
    line_u, line_u_half, q_z = run(
        functools.partial(chain_u_kernel, 2), [U_SHAPE, U_HALF, FULL], U_SLOTS, 6, s, *s_z, u, *u_z, after=(line_s,)
    )

    u_x = ring(1, line_u, line_u_half)
    s_x = exchanged(*s_x)
    ap, o, packed = run(own_kernel, [FULL, FULL, S_SHAPE], [(FULL, BF16), (FULL, BF16), (FULL, F32)], 3, s, l, u, g, p_z, q_z)
    plane_s, _, p_x = run(functools.partial(chain_s_kernel, 1), [S_SHAPE, S_HALF, FULL], S_SLOTS, 3, line_s, *s_x)
    s_y = send(plane_s, moved(0, (1, 2)))
    before = send(packed, NEXT)
    u_x = exchanged(*u_x)
    plane_u, plane_u_half, q_x = run(
        functools.partial(chain_u_kernel, 1),
        [U_SHAPE, U_HALF, FULL],
        U_SLOTS,
        6,
        line_s, *s_x, line_u, *u_x,
        after=(ap,),
    )

    u_y = ring(0, plane_u, plane_u_half)
    s_y_other = send(s_y, CORES)
    u_1, u_1_other, u_2, u_2_other = exchanged(*u_y)
    acc, r1, r2, r3 = run(reach_kernel, [FULL] * 4, [(FULL, F32)] * 2, 5, o, ap, p_x, q_x, s_y, s_y_other)
    return tuple(
        run(
            last_kernel,
            [(1, B, B), (1, B, B)],
            [(FULL, F32), (FULL, F32), (U_SHAPE, F32)],
            7,
            acc, r1, r2, r3, u_1, u_1_other, u_2, u_2_other, before,
        )
    )


def solution(mesh):
    spec = P(TM, None, None)
    return jax.shard_map(local, mesh=mesh, in_specs=(spec, spec), out_specs=(spec, spec), check_vma=False)
```

```python
import functools

import jax
import jax.numpy as jnp
from jax import lax
from jax.experimental import pallas as pl
from jax.experimental.pallas import tpu as pltpu
from jax.sharding import PartitionSpec as P

TM = "tm"
F32 = jnp.float32
BF16 = jnp.bfloat16
B = 320
S_ROWS = 800
U_ROWS = 544


def index(y, x, z, core):
    return ((y * 4 + x) * 4 + z) * 2 + core


def moved(axis, k_of_core):
    pairs = []
    for y in range(4):
        for x in range(4):
            for z in range(4):
                for core in range(2):
                    there = [y, x, z]
                    there[axis] = (there[axis] + k_of_core[core]) % 4
                    pairs.append((index(*there, core), index(y, x, z, core)))
    return pairs


CORES = [(i, i ^ 1) for i in range(128)]
NEXT = [(i, (i + 1) % 128) for i in range(128)]


def send(value, pairs):
    return lax.ppermute(value, TM, pairs)


def split(a):
    high = a.astype(BF16)
    return high, (a - high.astype(F32)).astype(BF16)


def product(a, b):
    (ah, al), (bh, bl) = a, b
    return lax.dot_general(
        jnp.concatenate([ah, ah, al], axis=1),
        jnp.concatenate([bh, bl, bh], axis=0),
        (((1,), (0,)), ((), ())),
        preferred_element_type=F32,
    )


def product_t(a, b):
    (ah, al), (bh, bl) = a, b
    return lax.dot_general(
        jnp.concatenate([ah, ah, al], axis=1),
        jnp.concatenate([bh, bl, bh], axis=1),
        (((1,), (1,)), ((), ())),
        preferred_element_type=F32,
    )


def sandwich(a, middle):
    return product_t(split(product(a, split(middle))), a)


def unpack_s(ref):
    tail = ref[640:800, :]
    tail = jnp.concatenate([tail[:, :64], tail[:, 64:]], axis=0)
    return jnp.concatenate([ref[0:320, :], ref[320:640, :], tail], axis=1)


def pack_s(ref, a):
    ref[0:320, :] = a[:, 0:128]
    ref[320:640, :] = a[:, 128:256]
    ref[640:800, :] = jnp.concatenate([a[0:160, 256:320], a[160:320, 256:320]], axis=1)


def zeros(rows, columns):
    return jnp.zeros((rows, columns), F32)


def unpack_u(ref):
    b2 = ref[384:512, :]
    c2 = ref[512:544, :]
    c2 = jnp.concatenate([c2[:, :64], c2[:, 64:]], axis=0)
    top = jnp.concatenate([ref[0:128, :], ref[128:256, :], b2[:, :64]], axis=1)
    mid = jnp.concatenate([zeros(128, 128), ref[256:384, :], b2[:, 64:]], axis=1)
    low = jnp.concatenate([zeros(64, 256), c2], axis=1)
    return jnp.concatenate([top, mid, low], axis=0)


def upper_of(g):
    top = jnp.concatenate([0.5 * g[0:128, 0:128], g[0:128, 128:320]], axis=1)
    mid = jnp.concatenate([zeros(128, 128), 0.5 * g[128:256, 128:256], g[128:256, 256:320]], axis=1)
    low = jnp.concatenate([zeros(64, 256), 0.5 * g[256:320, 256:320]], axis=1)
    return jnp.concatenate([top, mid, low], axis=0)


def pack_u(ref, z):
    ref[0:128, :] = z[0:128, 0:128]
    ref[128:256, :] = z[0:128, 128:256] + z[128:256, 0:128].T
    ref[256:384, :] = z[128:256, 128:256]
    b02 = z[0:128, 256:320] + z[256:320, 0:128].T
    b12 = z[128:256, 256:320] + z[256:320, 128:256].T
    ref[384:512, :] = jnp.concatenate([b02, b12], axis=1)
    c = z[256:320, 256:320]
    ref[512:544, :] = jnp.concatenate([c[0:32], c[32:64]], axis=1)


def core_index():
    return lax.rem(lax.axis_index(TM), 2)


def place(axis):
    return lax.rem(lax.div(lax.axis_index(TM), (32, 8, 2)[axis]), 4)


def half_of(ref, rows):
    return ref[pl.ds(pl.multiple_of(core_index() * (rows // 2), 8), rows // 2), :]


def join(out, mine, other):
    rows = mine.shape[0]
    core = core_index()
    out[pl.ds(pl.multiple_of(core * rows, 8), rows), :] = mine[...]
    out[pl.ds(pl.multiple_of((1 - core) * rows, 8), rows), :] = other[...]


def ring_slots(axis):
    here = place(axis)
    turn = 2 * core_index()
    return [lax.rem(here + k, 4) for k in (0, 1 + turn, 3 - turn, 2)]


def pair_kernel(l_ref, l_other_ref, g_ref, g_other_ref, s_ref, u_ref, half_ref):
    core = core_index()
    own, other = l_ref[...], l_other_ref[...]
    first = split(jnp.where(core == 0, own, other))
    second = split(jnp.where(core == 0, other, own))
    pack_s(s_ref, product(first, second))
    half_ref[: S_ROWS // 2, :] = half_of(s_ref, S_ROWS)
    own, other = g_ref[...], g_other_ref[...]
    start = jnp.where(core == 0, own, other)
    later = jnp.where(core == 0, other, own)
    pack_u(u_ref, upper_of(start) + sandwich(first, upper_of(later)))
    half_ref[S_ROWS // 2 :, :] = half_of(u_ref, U_ROWS)


def load_s(axis, s, mine, other, mine_half, other_half, high, low, whole):
    join(whole, mine_half.at[pl.ds(0, S_ROWS // 2)], other_half.at[pl.ds(0, S_ROWS // 2)])
    other = other.at[pl.ds(other.shape[0] - S_ROWS, S_ROWS)]
    for slot, ref in zip(ring_slots(axis), (s, mine, other, whole)):
        high[slot], low[slot] = split(unpack_s(ref))


def chain_s_kernel(axis, s0, s1, s2, s3, s4, *refs):
    total_ref, half_ref, after_ref, high, low, whole = refs[-6:]
    load_s(axis, s0, s1, s2, s3, s4, high, low, whole)
    here = place(axis)
    running = None
    for slot in (3, 2, 1, 0):
        factor = (high[slot], low[slot])
        if running is None:
            running = high[slot].astype(F32) + low[slot].astype(F32)
            row = lax.broadcasted_iota(jnp.int32, (B, B), 0)
            column = lax.broadcasted_iota(jnp.int32, (B, B), 1)

            @pl.when(here == 3)
            def _():
                after_ref[...] = jnp.where(row == column, 1.0, 0.0).astype(F32)
        else:
            running = product(factor, split(running))
        if slot > 0:
            kept = running

            @pl.when(here == slot - 1)
            def _():
                after_ref[...] = kept

    pack_s(total_ref, running)
    half_ref[...] = half_of(total_ref, S_ROWS)


def chain_u_kernel(axis, s0, s1, s2, s3, s4, u0, u1, u2, u3, u4, *refs):
    total_ref, half_ref, after_ref, high, low, whole, middle, whole_u = refs[-8:]
    load_s(axis, s0, s1, s2, s3, s4, high, low, whole)
    last = pl.ds(u3.shape[0] - U_ROWS // 2, U_ROWS // 2)
    join(whole_u, u3.at[last], u4.at[last])
    for slot, ref in zip(ring_slots(axis), (u0, u1, u2, whole_u)):
        middle[slot] = unpack_u(ref)
    here = place(axis)

    @pl.when(here == 3)
    def _():
        after_ref[...] = jnp.zeros((B, B), F32)

    running = middle[3]
    for slot in (2, 1, 0):
        kept = running

        @pl.when(here == slot)
        def _():
            after_ref[...] = kept

        running = middle[slot] + sandwich((high[slot], low[slot]), running)
    pack_u(total_ref, running)
    half_ref[...] = half_of(total_ref, U_ROWS)


def gather_kernel(half_ref, whole_ref, *refs):
    out_ref = refs[-1]
    out_ref[: S_ROWS // 2, :] = half_ref[...]
    out_ref[S_ROWS // 2 :, :] = whole_ref[...]


def own_kernel(s_ref, l_ref, u_ref, g_ref, p_ref, z_ref, ap_ref, o_ref, packed_ref, high, low, base):
    core = core_index()
    pack_s(packed_ref, l_ref[...])

    @pl.when(core == 0)
    def _():
        high[...], low[...] = split(unpack_s(s_ref))
        base[...] = unpack_u(u_ref)

    @pl.when(core != 0)
    def _():
        high[...], low[...] = split(l_ref[...])
        base[...] = upper_of(g_ref[...])

    a = (high[...], low[...])
    ap_ref[...] = product(a, split(p_ref[...]))
    o_ref[...] = base[...] + sandwich(a, z_ref[...])


def reach_kernel(o_ref, ap_ref, p_ref, z_ref, acc_ref, r1_ref):
    ap = split(ap_ref[...])
    acc_ref[...] = o_ref[...] + sandwich(ap, z_ref[...])
    r1_ref[...] = jnp.where(place(0) < 3, product(ap, split(p_ref[...])), 0.0)


def gather_y_kernel(s_ref, whole_ref, half_ref, *refs):
    out_ref = refs[-1]
    out_ref[:S_ROWS, :] = s_ref[...]
    out_ref[S_ROWS : S_ROWS + U_ROWS, :] = whole_ref[...]
    out_ref[S_ROWS + U_ROWS :, :] = half_ref[...]


def last_kernel(acc_ref, r1_ref, s_mine, mine_ref, mine_half, other_ref, before_ref, x_ref, c_ref, a, b, u, w, whole):
    core = core_index()
    y = place(0)
    s_other = other_ref.at[pl.ds(0, S_ROWS)]
    u_other = other_ref.at[pl.ds(S_ROWS, U_ROWS)]

    @pl.when(core == 0)
    def _():
        a[...] = unpack_s(s_mine)
        b[...] = unpack_s(s_other)
        u[...] = unpack_u(mine_ref)
        w[...] = unpack_u(u_other)

    @pl.when(core != 0)
    def _():
        a[...] = unpack_s(s_other)
        b[...] = unpack_s(s_mine)
        u[...] = unpack_u(u_other)
        w[...] = unpack_u(mine_ref)

    join(whole, mine_half, other_ref.at[pl.ds(S_ROWS + U_ROWS, U_ROWS // 2)])
    r1 = split(r1_ref[...])
    r2 = split(jnp.where(y < 2, product(r1, split(a[...])), 0.0))
    r3 = split(jnp.where(y < 1, product(r2, split(b[...])), 0.0))
    half = acc_ref[...] + sandwich(r1, u[...]) + sandwich(r2, unpack_u(whole)) + sandwich(r3, w[...])
    x = half + half.T
    x_ref[0] = x
    before = jnp.where(lax.axis_index(TM) > 0, unpack_s(before_ref), 0.0)
    c_ref[0] = product_t(split(x), split(before))


def run(kernel, shapes, scratch, products, *operands, after=()):
    size = sum(o.size for o in operands) * 4
    specs = [pl.BlockSpec(memory_space=pltpu.VMEM)] * len(operands) + [pl.BlockSpec(memory_space=pl.ANY)] * len(after)
    return pl.pallas_call(
        kernel,
        in_specs=specs,
        out_shape=[jax.ShapeDtypeStruct(s, F32) for s in shapes],
        scratch_shapes=[pltpu.VMEM(s, d) for s, d in scratch],
        compiler_params=pltpu.CompilerParams(vmem_limit_bytes=32 * 1024 * 1024),
        cost_estimate=pl.CostEstimate(flops=10**9, bytes_accessed=10**7, transcendentals=0),
    )(*operands, *after)


S_SHAPE = (S_ROWS, 128)
S_HALF = (S_ROWS // 2, 128)
U_SHAPE = (U_ROWS, 128)
U_HALF = (U_ROWS // 2, 128)
SU_HALF = ((S_ROWS + U_ROWS) // 2, 128)
FULL = (B, B)
S_SLOTS = [((4, B, B), BF16), ((4, B, B), BF16), (S_SHAPE, F32)]
U_SLOTS = S_SLOTS + [((4, B, B), F32), (U_SHAPE, F32)]


def ring(axis, whole, half):
    return send(whole, moved(axis, (1, 3))), send(half, moved(axis, (2, 2)))


def exchanged(mine, mine_half):
    return mine, send(mine, CORES), mine_half, send(mine_half, CORES)


def local(schur_inverse, sweep_factor):
    g, l = schur_inverse[0], sweep_factor[0]

    l_other = send(l, CORES)
    g_other = send(g, CORES)
    s, u, half = run(pair_kernel, [S_SHAPE, U_SHAPE, SU_HALF], [], 3, l, l_other, g, g_other)

    s_mine, half_mine, u_mine = send(s, moved(2, (1, 3))), send(half, moved(2, (2, 2))), send(u, moved(2, (1, 3)))
    s_other, half_other = send(s_mine, CORES), send(half_mine, CORES)
    s_z = s_mine, s_other, half_mine, half_other
    line_s, line_s_half, p_z = run(
        functools.partial(chain_s_kernel, 2), [S_SHAPE, S_HALF, FULL], S_SLOTS, 3, s, *s_z, after=()
    )
    s_x = ring(1, line_s, line_s_half)
    u_z = u_mine, send(u_mine, CORES), half_mine, half_other
    line_u, line_u_half, q_z = run(
        functools.partial(chain_u_kernel, 2), [U_SHAPE, U_HALF, FULL], U_SLOTS, 6, s, *s_z, u, *u_z, after=(line_s,)
    )

    u_x = ring(1, line_u, line_u_half)
    s_x_mine, s_x_half = s_x
    (gathered,) = run(gather_kernel, [(S_ROWS + S_ROWS // 2, 128)], [], 1, s_x_half, s_x_mine, after=(line_u, u_x[0]))
    s_x_other = send(gathered, CORES)
    s_x = s_x_mine, s_x_other, s_x_half, s_x_other
    ap, o, packed = run(own_kernel, [FULL, FULL, S_SHAPE], [(FULL, BF16), (FULL, BF16), (FULL, F32)], 3, s, l, u, g, p_z, q_z)
    plane_s, _, p_x = run(functools.partial(chain_s_kernel, 1), [S_SHAPE, S_HALF, FULL], S_SLOTS, 3, line_s, *s_x, after=())
    s_y = send(plane_s, moved(0, (1, 2)))
    before = send(packed, NEXT)
    u_x = exchanged(*u_x)
    plane_u, plane_u_half, q_x = run(
        functools.partial(chain_u_kernel, 1),
        [U_SHAPE, U_HALF, FULL],
        U_SLOTS,
        6,
        line_s, *s_x, line_u, *u_x,
        after=(ap,),
    )

    u_1, u_2 = ring(0, plane_u, plane_u_half)
    acc, r1 = run(reach_kernel, [FULL] * 2, [], 3, o, ap, p_x, q_x)
    rows = S_ROWS + U_ROWS + U_ROWS // 2
    (gathered,) = run(gather_y_kernel, [(rows, 128)], [], 1, s_y, u_1, u_2, after=(before,))
    return tuple(
        run(
            last_kernel,
            [(1, B, B), (1, B, B)],
            [(FULL, F32)] * 4 + [(U_SHAPE, F32)],
            9,
            acc, r1, s_y, u_1, u_2, send(gathered, CORES), before,
        )
    )


def solution(mesh):
    spec = P(TM, None, None)
    return jax.shard_map(local, mesh=mesh, in_specs=(spec, spec), out_specs=(spec, spec), check_vma=False)
```

```python
import functools

import jax
import jax.numpy as jnp
from jax import lax
from jax.experimental import pallas as pl
from jax.experimental.pallas import tpu as pltpu
from jax.sharding import PartitionSpec as P

TM = "tm"
F32 = jnp.float32
BF16 = jnp.bfloat16
B = 320
S_ROWS = 800
U_ROWS = 544


def index(y, x, z, core):
    return ((y * 4 + x) * 4 + z) * 2 + core


def moved(axis, k_of_core):
    pairs = []
    for y in range(4):
        for x in range(4):
            for z in range(4):
                for core in range(2):
                    there = [y, x, z]
                    there[axis] = (there[axis] + k_of_core[core]) % 4
                    pairs.append((index(*there, core), index(y, x, z, core)))
    return pairs


CORES = [(i, i ^ 1) for i in range(128)]
NEXT = [(i, (i + 1) % 128) for i in range(128)]


def send(value, pairs):
    return lax.ppermute(value, TM, pairs)


def split(a):
    high = a.astype(BF16)
    return high, (a - high.astype(F32)).astype(BF16)


def product(a, b):
    (ah, al), (bh, bl) = a, b
    return lax.dot_general(
        jnp.concatenate([ah, ah, al], axis=1),
        jnp.concatenate([bh, bl, bh], axis=0),
        (((1,), (0,)), ((), ())),
        preferred_element_type=F32,
    )


def product_t(a, b):
    (ah, al), (bh, bl) = a, b
    return lax.dot_general(
        jnp.concatenate([ah, ah, al], axis=1),
        jnp.concatenate([bh, bl, bh], axis=1),
        (((1,), (1,)), ((), ())),
        preferred_element_type=F32,
    )


def sandwich(a, middle):
    return product_t(split(product(a, split(middle))), a)


def unpack_s(ref):
    tail = ref[640:800, :]
    tail = jnp.concatenate([tail[:, :64], tail[:, 64:]], axis=0)
    return jnp.concatenate([ref[0:320, :], ref[320:640, :], tail], axis=1)


def pack_s(ref, a):
    ref[0:320, :] = a[:, 0:128]
    ref[320:640, :] = a[:, 128:256]
    ref[640:800, :] = jnp.concatenate([a[0:160, 256:320], a[160:320, 256:320]], axis=1)


def zeros(rows, columns):
    return jnp.zeros((rows, columns), F32)


def unpack_u(ref):
    b2 = ref[384:512, :]
    c2 = ref[512:544, :]
    c2 = jnp.concatenate([c2[:, :64], c2[:, 64:]], axis=0)
    top = jnp.concatenate([ref[0:128, :], ref[128:256, :], b2[:, :64]], axis=1)
    mid = jnp.concatenate([zeros(128, 128), ref[256:384, :], b2[:, 64:]], axis=1)
    low = jnp.concatenate([zeros(64, 256), c2], axis=1)
    return jnp.concatenate([top, mid, low], axis=0)


def upper_of(g):
    top = jnp.concatenate([0.5 * g[0:128, 0:128], g[0:128, 128:320]], axis=1)
    mid = jnp.concatenate([zeros(128, 128), 0.5 * g[128:256, 128:256], g[128:256, 256:320]], axis=1)
    low = jnp.concatenate([zeros(64, 256), 0.5 * g[256:320, 256:320]], axis=1)
    return jnp.concatenate([top, mid, low], axis=0)


def pack_u(ref, z):
    ref[0:128, :] = z[0:128, 0:128]
    ref[128:256, :] = z[0:128, 128:256] + z[128:256, 0:128].T
    ref[256:384, :] = z[128:256, 128:256]
    b02 = z[0:128, 256:320] + z[256:320, 0:128].T
    b12 = z[128:256, 256:320] + z[256:320, 128:256].T
    ref[384:512, :] = jnp.concatenate([b02, b12], axis=1)
    c = z[256:320, 256:320]
    ref[512:544, :] = jnp.concatenate([c[0:32], c[32:64]], axis=1)


def core_index():
    return lax.rem(lax.axis_index(TM), 2)


def place(axis):
    return lax.rem(lax.div(lax.axis_index(TM), (32, 8, 2)[axis]), 4)


def half_of(ref, rows):
    return ref[pl.ds(pl.multiple_of(core_index() * (rows // 2), 8), rows // 2), :]


def join(out, mine, other):
    rows = mine.shape[0]
    core = core_index()
    out[pl.ds(pl.multiple_of(core * rows, 8), rows), :] = mine[...]
    out[pl.ds(pl.multiple_of((1 - core) * rows, 8), rows), :] = other[...]


def ring_slots(axis):
    here = place(axis)
    turn = 2 * core_index()
    return [lax.rem(here + k, 4) for k in (0, 1 + turn, 3 - turn, 2)]


def pair_kernel(l_ref, l_other_ref, g_ref, g_other_ref, s_ref, u_ref, half_ref):
    core = core_index()
    own, other = l_ref[...], l_other_ref[...]
    first = split(jnp.where(core == 0, own, other))
    second = split(jnp.where(core == 0, other, own))
    pack_s(s_ref, product(first, second))
    half_ref[: S_ROWS // 2, :] = half_of(s_ref, S_ROWS)
    own, other = g_ref[...], g_other_ref[...]
    start = jnp.where(core == 0, own, other)
    later = jnp.where(core == 0, other, own)
    pack_u(u_ref, upper_of(start) + sandwich(first, upper_of(later)))
    half_ref[S_ROWS // 2 :, :] = half_of(u_ref, U_ROWS)


def load_s(axis, s, mine, other, mine_half, other_half, high, low, whole):
    join(whole, mine_half.at[pl.ds(0, S_ROWS // 2)], other_half.at[pl.ds(0, S_ROWS // 2)])
    other = other.at[pl.ds(other.shape[0] - S_ROWS, S_ROWS)]
    for slot, ref in zip(ring_slots(axis), (s, mine, other, whole)):
        high[slot], low[slot] = split(unpack_s(ref))


def chain_s_kernel(axis, s0, s1, s2, s3, s4, *refs):
    total_ref, half_ref, after_ref, high, low, whole = refs[-6:]
    load_s(axis, s0, s1, s2, s3, s4, high, low, whole)
    here = place(axis)
    running = None
    for slot in (3, 2, 1, 0):
        factor = (high[slot], low[slot])
        if running is None:
            running = high[slot].astype(F32) + low[slot].astype(F32)
            row = lax.broadcasted_iota(jnp.int32, (B, B), 0)
            column = lax.broadcasted_iota(jnp.int32, (B, B), 1)

            @pl.when(here == 3)
            def _():
                after_ref[...] = jnp.where(row == column, 1.0, 0.0).astype(F32)
        else:
            running = product(factor, split(running))
        if slot > 0:
            kept = running

            @pl.when(here == slot - 1)
            def _():
                after_ref[...] = kept

    pack_s(total_ref, running)
    half_ref[...] = half_of(total_ref, S_ROWS)


def chain_u_kernel(axis, s0, s1, s2, s3, s4, u0, u1, u2, u3, u4, *refs):
    total_ref, half_ref, after_ref, high, low, whole, middle, whole_u = refs[-8:]
    load_s(axis, s0, s1, s2, s3, s4, high, low, whole)
    last = pl.ds(u3.shape[0] - U_ROWS // 2, U_ROWS // 2)
    join(whole_u, u3.at[last], u4.at[last])
    for slot, ref in zip(ring_slots(axis), (u0, u1, u2, whole_u)):
        middle[slot] = unpack_u(ref)
    here = place(axis)

    @pl.when(here == 3)
    def _():
        after_ref[...] = jnp.zeros((B, B), F32)

    running = middle[3]
    for slot in (2, 1, 0):
        kept = running

        @pl.when(here == slot)
        def _():
            after_ref[...] = kept

        running = middle[slot] + sandwich((high[slot], low[slot]), running)
    pack_u(total_ref, running)
    half_ref[...] = half_of(total_ref, U_ROWS)


def gather_kernel(half_ref, whole_ref, *refs):
    out_ref = refs[-1]
    out_ref[: S_ROWS // 2, :] = half_ref[...]
    out_ref[S_ROWS // 2 :, :] = whole_ref[...]


def own_kernel(s_ref, l_ref, u_ref, g_ref, p_ref, z_ref, *refs):
    ap_ref, o_ref, packed_ref, high, low, base = refs[-6:]
    core = core_index()
    pack_s(packed_ref, l_ref[...])

    @pl.when(core == 0)
    def _():
        high[...], low[...] = split(unpack_s(s_ref))
        base[...] = unpack_u(u_ref)

    @pl.when(core != 0)
    def _():
        high[...], low[...] = split(l_ref[...])
        base[...] = upper_of(g_ref[...])

    a = (high[...], low[...])
    ap_ref[...] = product(a, split(p_ref[...]))
    o_ref[...] = base[...] + sandwich(a, z_ref[...])


def reach_kernel(o_ref, ap_ref, p_ref, z_ref, mine_ref, other_ref, acc_ref, r1_ref, r2_ref, r3_ref, a, b):
    core = core_index()
    y = place(0)

    @pl.when(core == 0)
    def _():
        a[...] = unpack_s(mine_ref)
        b[...] = unpack_s(other_ref)

    @pl.when(core != 0)
    def _():
        a[...] = unpack_s(other_ref)
        b[...] = unpack_s(mine_ref)

    ap = split(ap_ref[...])
    acc_ref[...] = o_ref[...] + sandwich(ap, z_ref[...])
    r1 = jnp.where(y < 3, product(ap, split(p_ref[...])), 0.0)
    r2 = jnp.where(y < 2, product(split(r1), split(a[...])), 0.0)
    r3 = jnp.where(y < 1, product(split(r2), split(b[...])), 0.0)
    r1_ref[...] = r1
    r2_ref[...] = r2
    r3_ref[...] = r3


def last_kernel(acc_ref, r1_ref, r2_ref, r3_ref, mine_ref, other_ref, mine_half, other_half, before_ref, x_ref, c_ref, u, w, whole):
    core = core_index()

    @pl.when(core == 0)
    def _():
        u[...] = unpack_u(mine_ref)
        w[...] = unpack_u(other_ref)

    @pl.when(core != 0)
    def _():
        u[...] = unpack_u(other_ref)
        w[...] = unpack_u(mine_ref)

    join(whole, mine_half, other_half)
    half = acc_ref[...] + sandwich(split(r1_ref[...]), u[...]) + sandwich(split(r3_ref[...]), w[...])
    half = half + sandwich(split(r2_ref[...]), unpack_u(whole))
    x = half + half.T
    x_ref[0] = x
    before = jnp.where(lax.axis_index(TM) > 0, unpack_s(before_ref), 0.0)
    c_ref[0] = product_t(split(x), split(before))


def run(kernel, shapes, scratch, products, *operands, after=()):
    size = sum(o.size for o in operands) * 4
    specs = [pl.BlockSpec(memory_space=pltpu.VMEM)] * len(operands) + [pl.BlockSpec(memory_space=pl.ANY)] * len(after)
    return pl.pallas_call(
        kernel,
        in_specs=specs,
        out_shape=[jax.ShapeDtypeStruct(s, F32) for s in shapes],
        scratch_shapes=[pltpu.VMEM(s, d) for s, d in scratch],
        compiler_params=pltpu.CompilerParams(vmem_limit_bytes=32 * 1024 * 1024),
        cost_estimate=pl.CostEstimate(flops=10**9, bytes_accessed=10**7, transcendentals=0),
    )(*operands, *after)


S_SHAPE = (S_ROWS, 128)
S_HALF = (S_ROWS // 2, 128)
U_SHAPE = (U_ROWS, 128)
U_HALF = (U_ROWS // 2, 128)
SU_HALF = ((S_ROWS + U_ROWS) // 2, 128)
FULL = (B, B)
S_SLOTS = [((4, B, B), BF16), ((4, B, B), BF16), (S_SHAPE, F32)]
U_SLOTS = S_SLOTS + [((4, B, B), F32), (U_SHAPE, F32)]


def ring(axis, whole, half):
    return send(whole, moved(axis, (1, 3))), send(half, moved(axis, (2, 2)))


def exchanged(mine, mine_half):
    return mine, send(mine, CORES), mine_half, send(mine_half, CORES)


def local(schur_inverse, sweep_factor):
    g, l = schur_inverse[0], sweep_factor[0]

    l_other = send(l, CORES)
    g_other = send(g, CORES)
    s, u, half = run(pair_kernel, [S_SHAPE, U_SHAPE, SU_HALF], [], 3, l, l_other, g, g_other)

    s_mine, half_mine, u_mine = send(s, moved(2, (1, 3))), send(half, moved(2, (2, 2))), send(u, moved(2, (1, 3)))
    s_other, half_other = send(s_mine, CORES), send(half_mine, CORES)
    s_z = s_mine, s_other, half_mine, half_other
    line_s, line_s_half, p_z = run(
        functools.partial(chain_s_kernel, 2), [S_SHAPE, S_HALF, FULL], S_SLOTS, 3, s, *s_z, after=()
    )
    s_x = ring(1, line_s, line_s_half)
    u_z = u_mine, send(u_mine, CORES), half_mine, half_other
    line_u, line_u_half, q_z = run(
        functools.partial(chain_u_kernel, 2), [U_SHAPE, U_HALF, FULL], U_SLOTS, 6, s, *s_z, u, *u_z, after=(line_s,)
    )

    u_x = ring(1, line_u, line_u_half)
    s_x_mine, s_x_half = s_x
    (gathered,) = run(gather_kernel, [(S_ROWS + S_ROWS // 2, 128)], [], 1, s_x_half, s_x_mine, after=(line_u, u_x[0]))
    s_x_other = send(gathered, CORES)
    s_x = s_x_mine, s_x_other, s_x_half, s_x_other
    plane_s, _, p_x = run(functools.partial(chain_s_kernel, 1), [S_SHAPE, S_HALF, FULL], S_SLOTS, 3, line_s, *s_x, after=())
    s_y = send(plane_s, moved(0, (1, 2)))
    u_x = exchanged(*u_x)
    plane_u, plane_u_half, q_x = run(
        functools.partial(chain_u_kernel, 1),
        [U_SHAPE, U_HALF, FULL],
        U_SLOTS,
        6,
        line_s, *s_x, line_u, *u_x,
        after=(),
    )

    u_y = ring(0, plane_u, plane_u_half)
    ap, o, packed = run(own_kernel, [FULL, FULL, S_SHAPE], [(FULL, BF16), (FULL, BF16), (FULL, F32)], 3, s, l, u, g, p_z, q_z, after=(plane_u,))
    before = send(packed, NEXT)
    s_y_other = send(s_y, CORES)
    u_1, u_1_other, u_2, u_2_other = exchanged(*u_y)
    acc, r1, r2, r3 = run(reach_kernel, [FULL] * 4, [(FULL, F32)] * 2, 5, o, ap, p_x, q_x, s_y, s_y_other)
    return tuple(
        run(
            last_kernel,
            [(1, B, B), (1, B, B)],
            [(FULL, F32), (FULL, F32), (U_SHAPE, F32)],
            7,
            acc, r1, r2, r3, u_1, u_1_other, u_2, u_2_other, before,
        )
    )


def solution(mesh):
    spec = P(TM, None, None)
    return jax.shard_map(local, mesh=mesh, in_specs=(spec, spec), out_specs=(spec, spec), check_vma=False)
```
